32 devices in a mesh: parts: 2 (over x), tensor: 16 (over z, y, core).
Axes of the slice: x: 2, y: 2, z: 4, core: 2. Of those that a mesh axis runs over, the one named last changes fastest.
Arguments:
- activations: bfloat16 [256, 8192], P(('parts', 'tensor')), parts along dimension 0, may hold values from -6 to 6
- out_grad: bfloat16 [256, 8192], P(('parts', 'tensor')), parts along dimension 0, may hold values from -6 to 6
- loss_mask: int32 [256], P(('parts', 'tensor')), parts along dimension 0, may hold values 0 or 1
- w_gate: bfloat16 [8192, 14336], P(None, 'tensor'), may hold values from -0.0625 to 0.0625
- w_down: bfloat16 [14336, 8192], P('tensor'), may hold values from -0.046875 to 0.046875
- basis_a: bfloat16 [8192, 8192], P('tensor'), may hold values from -0.0625 to 0.0625
- basis_g: bfloat16 [14336, 14336], P('tensor'), may hold values from -0.0625 to 0.0625
Outputs:
- eigenvalues: float32 [16384, 14336], P('parts', 'tensor'), parts along dimension 0
The draws below stay inside these ranges and needn't reach their ends.
There are 2 independent parts, one for each index of `parts`. The reference program is written for one: setup_inputs(seed, part) draws one part's arguments, and reference() takes and returns one part's arrays. A program takes and returns all parts, laid end to end along the dimension named above; an argument that names none is the same for every part. Nothing has to cross between parts.
All inputs are finite; a program needn't handle non-finite values. No bound on the sum of `loss_mask` on one device may be relied on, other than what follows from the above.
Results may differ from the reference program's by a relative error of at most 0.0064.
Values may be sent and summed in bfloat16 or wider, within the bound.
No kernel may reach another device: no remote copies, remote signals or barrier semaphores. Data moves between devices by JAX's collectives and lax.ppermute only.
A program may use at most 256 MiB of HBM per device.

```python
import jax
import jax.numpy as jnp

D = 8192
FF = 14336
SEQS = 2
SEQ = 64
TOKENS = 128


def with_ends(result, own_key, low, high):
    longest = result.shape.index(max(result.shape))
    spots = []
    for shift in (0, 1):
        where = [jax.random.randint(jax.random.fold_in(own_key, axis), (), 0, length) for axis, length in enumerate(result.shape)]
        where[longest] = (where[longest] + shift) % result.shape[longest]
        spots.append(tuple(where))
    return result.at[spots[0]].set(low).at[spots[1]].set(high)


def with_spikes(values, stream_key, source, target, blocks, factor):
    def block_of(position):
        return (jnp.arange(values.shape[position]) // (values.shape[position] // blocks)).reshape((-1,) + (1,) * (values.ndim - 1 - position))

    first = jax.random.permutation(stream_key, blocks)[block_of(target)]
    second = (block_of(target) + blocks // 2) % blocks
    return jnp.where((block_of(source) == first) | (block_of(source) == second), factor * values, values)


def levels(stream_key, dims, pieces, smallest, top_value):
    level = 1.0
    for dim, shards_of in pieces:
        draws = jax.random.uniform(jax.random.fold_in(jax.random.fold_in(stream_key, 6), dim), (shards_of,), jnp.float32, smallest / len(pieces), top_value / len(pieces))
        level = level * jnp.repeat(jnp.exp(draws), dims[dim] // shards_of).reshape((-1,) + (1,) * (len(dims) - 1 - dim))
    return level


def gaussian(stream_key, dims, width, most, pieces=(), kind=jnp.bfloat16):
    loudness = levels(stream_key, dims, pieces, -0.22, 0.18) if pieces else 1.0
    result = jax.random.normal(stream_key, dims, jnp.float32) * width * loudness
    return jnp.minimum(jnp.maximum(result, -most), most).astype(kind)


def gaussian_with(key, extent, scale, limit, pieces, heavy, held_as=jnp.bfloat16):
    entries = scale * jax.random.normal(key, extent, jnp.float32)
    if pieces:
        entries = entries * levels(key, extent, pieces, -0.22, 0.18)
    return jnp.clip(with_spikes(entries, jax.random.fold_in(key, 3), *heavy), -limit, limit).astype(held_as)


def setup_inputs(seed: int = 0, part: int = 0) -> dict:
    keys = jax.random.split(jax.random.key(seed), 8)
    part_keys = jax.random.split(jax.random.fold_in(keys[7], part), 8)
    activations = gaussian(part_keys[0], (TOKENS, D), 1.0, 6.0, ((0, 16),))
    out_grad = gaussian(part_keys[1], (TOKENS, D), 1.0, 6.0, ((0, 16),))
    loss_mask = with_ends((jax.random.randint(part_keys[2], (TOKENS,), 0, 4) < 3).astype(jnp.int32), jax.random.fold_in(part_keys[2], 1), 0, 1)
    w_gate = gaussian(keys[3], (D, FF), D ** -0.5, 0.0625, ((1, 16),))
    w_down = gaussian(keys[4], (FF, D), FF ** -0.5, 0.046875, ((0, 16),))
    basis_a = gaussian(keys[5], (D, D), D ** -0.5, 0.0625, ((0, 16),))
    basis_g = gaussian_with(keys[6], (FF, FF), FF ** -0.5, 0.0625, ((0, 16),), (0, 1, 16, 2.0))
    return {"activations": activations, "out_grad": out_grad, "loss_mask": loss_mask, "w_gate": w_gate, "w_down": w_down, "basis_a": basis_a, "basis_g": basis_g}


def reference(activations, out_grad, loss_mask, w_gate, w_down, basis_a, basis_g):
    masked = out_grad * loss_mask.astype(out_grad.dtype)[:, None]
    gate_pre = jnp.dot(activations, w_gate, preferred_element_type=jnp.float32)
    hid_grad = jnp.dot(masked, w_down.T, preferred_element_type=jnp.float32)
    up_grad = (hid_grad * jax.nn.silu(gate_pre)).astype(jnp.bfloat16)
    proj_a = jnp.dot(activations, basis_a, preferred_element_type=jnp.float32).astype(jnp.bfloat16)
    proj_g = jnp.dot(up_grad, basis_g, preferred_element_type=jnp.float32).astype(jnp.bfloat16)
    total = jnp.zeros((D, FF), jnp.float32)
    for which in range(SEQS):
        rows_a = proj_a[which * SEQ:(which + 1) * SEQ]
        rows_g = proj_g[which * SEQ:(which + 1) * SEQ]
        product = jnp.dot(rows_a.T, rows_g, preferred_element_type=jnp.float32)
        total = total + product * product
    return total / (SEQS * SEQ)
```

```python
import functools

import jax
import jax.numpy as jnp
from jax import lax
from jax.experimental import pallas as pl
from jax.experimental.pallas import tpu as pltpu
from jax.sharding import Mesh
from jax.sharding import PartitionSpec as P

SEQS = 2
F32 = jnp.float32
BF16 = jnp.bfloat16
VMEM_LIMIT = 48 * 1024 * 1024


def params():
    return pltpu.CompilerParams(vmem_limit_bytes=VMEM_LIMIT)


def plain(activations, out_grad, loss_mask, w_gate, w_down, basis_a, basis_g):
    axes = ("z", "y", "core")
    masked = out_grad * loss_mask.astype(out_grad.dtype)[:, None]
    whole_act = lax.all_gather(activations, axes, axis=0, tiled=True)
    whole_grad = lax.all_gather(masked, axes, axis=0, tiled=True)
    gate_pre = jnp.dot(whole_act, w_gate, preferred_element_type=F32)
    hid_grad = lax.dot_general(
        whole_grad, w_down, (((1,), (1,)), ((), ())), preferred_element_type=F32
    )
    up_grad = (hid_grad * jax.nn.silu(gate_pre)).astype(BF16)
    depth = basis_a.shape[0]
    own_act = lax.dynamic_slice_in_dim(whole_act, lax.axis_index(axes) * depth, depth, axis=1)
    share_a = lax.psum_scatter(
        jnp.dot(own_act, basis_a, preferred_element_type=F32),
        axes,
        scatter_dimension=1,
        tiled=True,
    ).astype(BF16)
    proj_a = lax.all_gather(share_a, axes, axis=1, tiled=True)
    proj_g_cols = lax.psum_scatter(
        lax.dot_general(basis_g, up_grad, (((0,), (1,)), ((), ())), preferred_element_type=F32),
        axes,
        scatter_dimension=0,
        tiled=True,
    ).astype(BF16)
    tokens = proj_a.shape[0]
    seq = tokens // SEQS
    total = 0.0
    for which in range(SEQS):
        rows = slice(which * seq, (which + 1) * seq)
        product = lax.dot_general(
            proj_a[rows],
            proj_g_cols[:, rows],
            (((0,), (1,)), ((), ())),
            preferred_element_type=F32,
        )
        total = total + product * product
    return total / tokens


def assemble(place, pieces, whole):
    part = pieces[0].shape[0] // SEQS
    for other in range(2):
        for across in range(2):
            core = (place[2] + other) % 2
            y = (place[1] + across) % 2
            for which in range(SEQS):
                start = ((which * 2 + core) * 2 + y) * part
                whole[pl.ds(pl.multiple_of(start, part), part), :] = pieces[other * 2 + across][
                    which * part : (which + 1) * part, :
                ]


def gate_kernel(place, p0, p1, p2, p3, weight, out, whole):
    assemble(place, (p0, p1, p2, p3), whole)
    product = jnp.dot(whole[...], weight[...], preferred_element_type=F32)

    @pl.when(pl.program_id(0) == 0)
    def _():
        out[...] = product

    @pl.when(pl.program_id(0) > 0)
    def _():
        out[...] += product


def gate_product(place, pieces, weight, step):
    rows, depth = pieces[0].shape
    width = weight.shape[1]
    return pl.pallas_call(
        gate_kernel,
        grid_spec=pltpu.PrefetchScalarGridSpec(
            num_scalar_prefetch=1,
            grid=(depth // step,),
            in_specs=[pl.BlockSpec((rows, step), lambda k, s: (0, k))] * 4
            + [pl.BlockSpec((step, width), lambda k, s: (k, 0))],
            out_specs=pl.BlockSpec((4 * rows, width), lambda k, s: (0, 0)),
            scratch_shapes=[pltpu.VMEM((4 * rows, step), BF16)],
        ),
        out_shape=jax.ShapeDtypeStruct((4 * rows, width), F32),
        compiler_params=params(),
        name="gate",
    )(place, *pieces, weight)


def down_kernel(place, p0, p1, p2, p3, weight, gate, out, whole, total):
    assemble(place, (p0, p1, p2, p3), whole)
    product = lax.dot_general(
        whole[...], weight[...], (((1,), (1,)), ((), ())), preferred_element_type=F32
    )

    @pl.when(pl.program_id(0) == 0)
    def _():
        total[...] = product

    @pl.when(pl.program_id(0) > 0)
    def _():
        total[...] += product

    @pl.when(pl.program_id(0) == pl.num_programs(0) - 1)
    def _():
        pre = gate[...]
        out[...] = (total[...] * (pre / (1.0 + jnp.exp(-pre)))).astype(out.dtype)


def down_product(place, pieces, weight, gate, step):
    rows, depth = pieces[0].shape
    width = weight.shape[0]
    return pl.pallas_call(
        down_kernel,
        grid_spec=pltpu.PrefetchScalarGridSpec(
            num_scalar_prefetch=1,
            grid=(depth // step,),
            in_specs=[pl.BlockSpec((rows, step), lambda k, s: (0, k))] * 4
            + [
                pl.BlockSpec((width, step), lambda k, s: (0, k)),
                pl.BlockSpec((4 * rows, width), lambda k, s: (0, 0)),
            ],
            out_specs=pl.BlockSpec((4 * rows, width), lambda k, s: (0, 0)),
            scratch_shapes=[
                pltpu.VMEM((4 * rows, step), BF16),
                pltpu.VMEM((4 * rows, width), F32),
            ],
        ),
        out_shape=jax.ShapeDtypeStruct((4 * rows, width), BF16),
        compiler_params=params(),
        name="down",
    )(place, *pieces, weight, gate)


def share_a_kernel(place, p0, p1, p2, p3, basis, out, whole):
    @pl.when(pl.program_id(0) == 0)
    def _():
        assemble(place, (p0, p1, p2, p3), whole)

    out[0] = jnp.dot(whole[...], basis[...], preferred_element_type=F32).astype(out.dtype)


def share_a(place, pieces, basis, chips, flip, kind):
    rows = pieces[0].shape[0]
    depth, columns = basis.shape
    block = columns // (2 * chips)
    return pl.pallas_call(
        share_a_kernel,
        grid_spec=pltpu.PrefetchScalarGridSpec(
            num_scalar_prefetch=1,
            grid=(chips,),
            in_specs=[pl.BlockSpec((rows, depth), lambda j, s: (0, s[3]))] * 4
            + [pl.BlockSpec((depth, block), lambda j, s: (0, (s[2] + flip) % 2 * chips + j))],
            out_specs=pl.BlockSpec((1, 4 * rows, block), lambda j, s: (j, 0, 0)),
            scratch_shapes=[pltpu.VMEM((4 * rows, depth), BF16)],
        ),
        out_shape=jax.ShapeDtypeStruct((chips, 4 * rows, block), kind),
        compiler_params=params(),
        name="share_a",
    )(place, *pieces, basis)


def share_g_kernel(place, up, basis, out):
    out[0] = jnp.dot(up[...], basis[...], preferred_element_type=F32).astype(out.dtype)


def share_g(place, up, basis, chips, flip, kind):
    tokens, depth = up.shape
    block = basis.shape[1] // (2 * chips)
    return pl.pallas_call(
        share_g_kernel,
        grid_spec=pltpu.PrefetchScalarGridSpec(
            num_scalar_prefetch=1,
            grid=(chips,),
            in_specs=[
                pl.BlockSpec((tokens, depth), lambda j, s: (0, 0)),
                pl.BlockSpec((depth, block), lambda j, s: (0, 2 * j + (s[2] + flip) % 2)),
            ],
            out_specs=pl.BlockSpec((1, tokens, block), lambda j, s: (j, 0, 0)),
        ),
        out_shape=jax.ShapeDtypeStruct((chips, tokens, block), kind),
        compiler_params=params(),
        name="share_g",
    )(place, up, basis)


def final_kernel(layers, place, a0, a1, a2, a3, g, out):
    step = pl.program_id(0)
    tokens = g.shape[0]
    seq = tokens // SEQS
    for which, ref in enumerate((a0, a1, a2, a3)):

        @pl.when(step // layers == which)
        def _(ref=ref):
            block = ref[lax.rem(step, layers)]
            total = None
            for s in range(SEQS):
                rows = slice(s * seq, (s + 1) * seq)
                product = lax.dot_general(
                    block[rows],
                    g[rows, :],
                    (((0,), (0,)), ((), ())),
                    preferred_element_type=F32,
                )
                total = product * product if total is None else total + product * product
            out[...] = total * (1.0 / tokens)


def final_product(place, pieces, g):
    layers, tokens, block = pieces[0].shape
    width = g.shape[1]

    def where(j, s):
        piece = j // layers
        core = (s[2] + piece // 2) % 2
        y = (s[1] + piece) % 2
        return ((core * layers + j % layers) * 2 + y, 0)

    return pl.pallas_call(
        functools.partial(final_kernel, layers),
        grid_spec=pltpu.PrefetchScalarGridSpec(
            num_scalar_prefetch=1,
            grid=(4 * layers,),
            in_specs=[pl.BlockSpec((layers, tokens, block), lambda j, s: (0, 0, 0))] * 4
            + [pl.BlockSpec((tokens, width), lambda j, s: (0, 0))],
            out_specs=pl.BlockSpec((block, width), where),
        ),
        out_shape=jax.ShapeDtypeStruct((4 * layers * block, width), F32),
        compiler_params=params(),
        name="final",
    )(place, *pieces, g)


def turn(value, axis, size, by):
    return lax.ppermute(value, axis, [(i, (i + by) % size) for i in range(size)])


def gather(value, z, layers):
    pieces = [value] + [turn(value, "z", layers, by) for by in range(1, layers)]
    mine = jnp.stack([lax.select_n((z - i) % layers, *pieces) for i in range(layers)])
    across = turn(mine, "y", 2, 1)
    return mine, across, turn(mine, "core", 2, 1), turn(across, "core", 2, 1)


def pick(value, which):
    return lax.dynamic_index_in_dim(value, which, 0, keepdims=False)


def reduce_blocks(kept, got, z, y, layers):
    shape = (layers, 2) + kept.shape[1:]
    kept, got = kept.reshape(shape), got.reshape(shape)

    def both(which):
        return lax.dynamic_index_in_dim(kept, which, 1, keepdims=False) + (
            lax.dynamic_index_in_dim(got, which, 1, keepdims=False).astype(F32)
        )

    total = both(y) + turn(both(1 - y).astype(BF16), "y", 2, 1).astype(F32)
    own = pick(total, z)
    for by in range(1, layers):
        own = own + turn(pick(total, (z + by) % layers).astype(BF16), "z", layers, by).astype(F32)
    return own.astype(BF16)


def on_device(layers, activations, out_grad, loss_mask, w_gate, w_down, basis_a, basis_g):
    z, y, core = (lax.axis_index(name) for name in ("z", "y", "core"))
    chips = 2 * layers
    place = jnp.stack([z, y, core, lax.axis_index(("z", "y", "core"))]).astype(jnp.int32)
    masked = out_grad * loss_mask.astype(out_grad.dtype)[:, None]

    def flat(stacks):
        return [s.reshape(-1, s.shape[-1]) for s in stacks]

    act = flat(gather(activations, z, layers))
    grad = flat(gather(masked, z, layers))
    sent_a = share_a(place, act, basis_a, chips, 1, BF16)
    kept_a = share_a(place, act, basis_a, chips, 0, F32)
    own_a = reduce_blocks(kept_a, turn(sent_a, "core", 2, 1), z, y, layers)
    proj_a = gather(own_a, z, layers)
    gate = gate_product(place, act, w_gate, 1024)
    up = down_product(place, grad, w_down, gate, 1024)
    sent_g = share_g(place, up, basis_g, chips, 1, BF16)
    kept_g = share_g(place, up, basis_g, chips, 0, F32)
    own_g = reduce_blocks(kept_g, turn(sent_g, "core", 2, 1), z, y, layers)
    return final_product(place, proj_a, own_g)


def solution(mesh):
    tensor = mesh.shape["tensor"]
    chips = tensor // 2
    across = max(d for d in range(1, chips + 1) if chips % d == 0 and d * d <= chips)
    layers = chips // across
    fine = Mesh(
        mesh.devices.reshape(mesh.shape["parts"], layers, across, 2), ("parts", "z", "y", "core")
    )
    t = ("z", "y", "core")
    placed = (
        P(("parts",) + t, None),
        P(("parts",) + t, None),
        P(("parts",) + t),
        P(None, t),
        P(t, None),
        P(t, None),
        P(t, None),
    )

    def step(*args):
        rows = args[0].shape[0] // (mesh.shape["parts"] * tensor)
        small = across == 2 and layers * rows // SEQS == 16
        body = functools.partial(on_device, layers) if small else plain
        return jax.shard_map(
            body, mesh=fine, in_specs=placed, out_specs=P("parts", t), check_vma=False
        )(*args)

    return step
```

```python
import functools

import jax
import jax.numpy as jnp
from jax import lax
from jax.experimental import pallas as pl
from jax.experimental.pallas import tpu as pltpu
from jax.sharding import Mesh
from jax.sharding import PartitionSpec as P

SEQS = 2
F32 = jnp.float32
BF16 = jnp.bfloat16
VMEM_LIMIT = 52 * 1024 * 1024


def plain(activations, out_grad, loss_mask, w_gate, w_down, basis_a, basis_g):
    axes = ("z", "y", "core")
    masked = out_grad * loss_mask.astype(out_grad.dtype)[:, None]
    whole_act = lax.all_gather(activations, axes, axis=0, tiled=True)
    whole_grad = lax.all_gather(masked, axes, axis=0, tiled=True)
    gate_pre = jnp.dot(whole_act, w_gate, preferred_element_type=F32)
    hid_grad = lax.dot_general(
        whole_grad, w_down, (((1,), (1,)), ((), ())), preferred_element_type=F32
    )
    up_grad = (hid_grad * jax.nn.silu(gate_pre)).astype(BF16)
    depth = basis_a.shape[0]
    own_act = lax.dynamic_slice_in_dim(whole_act, lax.axis_index(axes) * depth, depth, axis=1)
    share_a = lax.psum_scatter(
        jnp.dot(own_act, basis_a, preferred_element_type=F32),
        axes,
        scatter_dimension=1,
        tiled=True,
    ).astype(BF16)
    proj_a = lax.all_gather(share_a, axes, axis=1, tiled=True)
    proj_g_cols = lax.psum_scatter(
        lax.dot_general(basis_g, up_grad, (((0,), (1,)), ((), ())), preferred_element_type=F32),
        axes,
        scatter_dimension=0,
        tiled=True,
    ).astype(BF16)
    tokens = proj_a.shape[0]
    seq = tokens // SEQS
    total = 0.0
    for which in range(SEQS):
        rows = slice(which * seq, (which + 1) * seq)
        product = lax.dot_general(
            proj_a[rows],
            proj_g_cols[:, rows],
            (((0,), (1,)), ((), ())),
            preferred_element_type=F32,
        )
        total = total + product * product
    return total / tokens


def in_hbm():
    return pl.BlockSpec(memory_space=pltpu.HBM)


def anywhere():
    return pl.BlockSpec(memory_space=pl.ANY)


def same(shape):
    return pl.BlockSpec(shape, lambda i, s: (0,) * len(shape))


def call(kernel, place, operands, in_specs, outs, out_specs, scratch, flops, moved, name, after=(), through=()):
    n_in, n_out, n_after, n_through = len(operands), len(outs), len(after), len(through)
    skip = n_in + n_after + n_through

    def body(place, *refs):
        rest = refs[skip : skip + n_out] + refs[skip + n_out + n_through :]
        kernel(place, *refs[:n_in], *rest)

    return pl.pallas_call(
        body,
        grid_spec=pltpu.PrefetchScalarGridSpec(
            num_scalar_prefetch=1,
            grid=(1,),
            in_specs=list(in_specs) + [anywhere()] * (n_after + n_through),
            out_specs=list(out_specs) + [anywhere()] * n_through,
            scratch_shapes=scratch,
        ),
        out_shape=list(outs) + [jax.ShapeDtypeStruct(t.shape, t.dtype) for t in through],
        input_output_aliases={1 + n_in + n_after + i: n_out + i for i in range(n_through)},
        compiler_params=pltpu.CompilerParams(vmem_limit_bytes=VMEM_LIMIT),
        cost_estimate=pl.CostEstimate(flops=flops, transcendentals=0, bytes_accessed=moved),
        name=name,
    )(place, *operands, *after, *through)


def hold(place, value, *after):
    return call(lambda place: None, place, (), [], [], [], [], 0, 0, "hold", after, (value,))[0]


def row_copies(place, pieces, start_column, columns, whole, sems):
    part = pieces[0].shape[0] // SEQS
    copies = []
    for other in range(2):
        for across in range(2):
            core = (place[2] + other) % 2
            y = (place[1] + across) % 2
            for which in range(SEQS):
                start = pl.multiple_of(((which * 2 + core) * 2 + y) * part, part)
                copies.append(
                    pltpu.make_async_copy(
                        pieces[other * 2 + across].at[
                            pl.ds(which * part, part), pl.ds(start_column, columns)
                        ],
                        whole.at[pl.ds(start, part), :],
                        sems.at[len(copies)],
                    )
                )
    return copies


def start_all(copies):
    for copy in copies:
        copy.start()


def wait_all(copies):
    for copy in copies:
        copy.wait()


def gate_kernel(steps, place, p0, p1, p2, p3, weight, out, whole, buffer, sems, row_sems):
    rows_in = row_copies(place, (p0, p1, p2, p3), 0, whole.shape[1], whole, row_sems)
    start_all(rows_in)
    depth = weight.shape[0] // steps
    copies = []
    for i in range(steps):
        rows = pl.ds(i * depth, depth)
        copies.append(pltpu.make_async_copy(weight.at[rows], buffer.at[rows], sems.at[i]))
    start_all(copies)
    wait_all(rows_in)
    total = None
    for i in range(steps):
        copies[i].wait()
        part = slice(i * depth, (i + 1) * depth)
        product = jnp.dot(whole[:, part], buffer[part, :], preferred_element_type=F32)
        total = product if total is None else total + product
    out[...] = total


def gate_product(place, pieces, weight, after, through, steps=8):
    rows, depth = pieces[0].shape
    width = weight.shape[1]
    return call(
        functools.partial(gate_kernel, steps),
        place,
        (*pieces, weight),
        [in_hbm()] * 5,
        [jax.ShapeDtypeStruct((4 * rows, width), F32)],
        [same((4 * rows, width))],
        [
            pltpu.VMEM((4 * rows, depth), BF16),
            pltpu.VMEM((depth, width), BF16),
            pltpu.SemaphoreType.DMA((steps,)),
            pltpu.SemaphoreType.DMA((4 * SEQS,)),
        ],
        8 * rows * depth * width,
        2 * depth * width,
        "gate",
        after=after,
        through=through,
    )


def down_kernel(steps, place, p0, p1, p2, p3, weight, gate, out, whole, buffer, sems, row_sems):
    rows_in = row_copies(place, (p0, p1, p2, p3), 0, whole.shape[1], whole, row_sems)
    start_all(rows_in)
    depth = weight.shape[1] // steps
    copies = []
    for i in range(steps):
        columns = pl.ds(i * depth, depth)
        copies.append(pltpu.make_async_copy(weight.at[:, columns], buffer.at[:, columns], sems.at[i]))
    start_all(copies)
    wait_all(rows_in)
    total = None
    for i in range(steps):
        copies[i].wait()
        part = slice(i * depth, (i + 1) * depth)
        product = lax.dot_general(
            whole[:, part], buffer[:, part], (((1,), (1,)), ((), ())), preferred_element_type=F32
        )
        total = product if total is None else total + product
    pre = gate[...]
    out[...] = (total * (pre / (1.0 + jnp.exp(-pre)))).astype(out.dtype)


def down_product(place, pieces, weight, gate, after, through, steps=8):
    rows, depth = pieces[0].shape
    width = weight.shape[0]
    return call(
        functools.partial(down_kernel, steps),
        place,
        (*pieces, weight, gate),
        [in_hbm()] * 5 + [same((4 * rows, width))],
        [jax.ShapeDtypeStruct((4 * rows, width), BF16)],
        [same((4 * rows, width))],
        [
            pltpu.VMEM((4 * rows, depth), BF16),
            pltpu.VMEM((width, depth), BF16),
            pltpu.SemaphoreType.DMA((steps,)),
            pltpu.SemaphoreType.DMA((4 * SEQS,)),
        ],
        8 * rows * depth * width,
        2 * depth * width,
        "down",
        after=after,
        through=through,
    )


def share_copies(place, basis, flip, block, buffer, sems):
    copies = []
    for chip in range(buffer.shape[0]):
        start = pl.multiple_of((2 * chip + (place[2] + flip) % 2) * block, block)
        copies.append(
            pltpu.make_async_copy(basis.at[:, pl.ds(start, block)], buffer.at[chip], sems.at[chip])
        )
    return copies


def share_products(left, copies, buffer, out):
    for chip, copy in enumerate(copies):
        copy.wait()
        out[chip] = jnp.dot(left[...], buffer[chip], preferred_element_type=F32).astype(out.dtype)


def share_a_kernel(block, place, p0, p1, p2, p3, basis, send, keep, left, buf0, buf1, sems, row_sems):
    depth = left.shape[1]
    start = pl.multiple_of(place[3] * depth, depth)
    rows_in = row_copies(place, (p0, p1, p2, p3), start, depth, left, row_sems)
    start_all(rows_in)
    sent = share_copies(place, basis, 1, block, buf0, sems.at[0])
    kept = share_copies(place, basis, 0, block, buf1, sems.at[1])
    start_all(sent)
    start_all(kept)
    wait_all(rows_in)
    share_products(left, sent, buf0, send)
    share_products(left, kept, buf1, keep)


def share_a(place, pieces, basis, chips, after):
    rows = pieces[0].shape[0]
    depth, columns = basis.shape
    block = columns // (2 * chips)
    shape = (chips, 4 * rows, block)
    return call(
        functools.partial(share_a_kernel, block),
        place,
        (*pieces, basis),
        [in_hbm()] * 5,
        [jax.ShapeDtypeStruct(shape, BF16), jax.ShapeDtypeStruct(shape, F32)],
        [same(shape), same(shape)],
        [pltpu.VMEM((4 * rows, depth), BF16)]
        + [pltpu.VMEM((chips, depth, block), BF16)] * 2
        + [pltpu.SemaphoreType.DMA((2, chips)), pltpu.SemaphoreType.DMA((4 * SEQS,))],
        8 * rows * depth * columns,
        2 * depth * columns,
        "share_a",
        after=after,
    )


def share_g_kernel(flip, block, place, up, basis, out, buffer, sems):
    copies = share_copies(place, basis, flip, block, buffer, sems)
    start_all(copies)
    share_products(up, copies, buffer, out)


def share_g(place, up, basis, chips, flip, kind, after, through):
    tokens, depth = up.shape
    block = basis.shape[1] // (2 * chips)
    shape = (chips, tokens, block)
    return call(
        functools.partial(share_g_kernel, flip, block),
        place,
        (up, basis),
        [same((tokens, depth)), in_hbm()],
        [jax.ShapeDtypeStruct(shape, kind)],
        [same(shape)],
        [pltpu.VMEM((chips, depth, block), BF16), pltpu.SemaphoreType.DMA((chips,))],
        2 * tokens * depth * chips * block,
        2 * depth * chips * block,
        "share_g",
        after=after,
        through=through,
    )


SLOTS = 8


def final_kernel(layers, first, place, a0, a1, a2, a3, g, out, pair, left, stage, sems, in_sems):
    pieces = (a0, a1, a2, a3)
    tokens, width = g.shape
    seq = tokens // SEQS
    block = stage.shape[1]
    loads = [
        pltpu.make_async_copy(pieces[which].at[z], left.at[which * layers + z], in_sems.at[which * layers + z])
        for which in range(4)
        for z in range(layers)
    ]
    start_all(loads)
    pair[...] = jnp.zeros_like(pair)
    for s in range(SEQS):
        rows = slice(s * seq, (s + 1) * seq)
        pair[rows, s * width : (s + 1) * width] = g[rows, :]
    copies = []
    for step in range(4 * layers):
        which, z = divmod(step, layers)
        core = (place[2] + which // 2) % 2
        y = (place[1] + which) % 2
        slot = step % SLOTS
        loads[step].wait()
        if step >= SLOTS:
            copies[step - SLOTS].wait()
        product = lax.dot_general(
            left[step], pair[...], (((0,), (0,)), ((), ())), preferred_element_type=F32
        )
        total = None
        for s in range(SEQS):
            one = product[:, s * width : (s + 1) * width]
            total = one * one if total is None else total + one * one
        stage[slot] = total * (1.0 / tokens)
        start = pl.multiple_of(((z * 2 + y) * 2 + core) * block, block)
        copies.append(
            pltpu.make_async_copy(
                stage.at[slot],
                out.at[pl.ds(start, block), pl.ds(first, width)],
                sems.at[slot],
            )
        )
        copies[step].start()
    wait_all(copies[-SLOTS:])


def final_product(place, pieces, g, first, columns, before):
    layers, tokens, block = pieces[0].shape
    width = g.shape[1]
    shape = jax.ShapeDtypeStruct((4 * layers * block, columns), F32)

    def kernel(place, a0, a1, a2, a3, g, *rest):
        final_kernel(layers, first, place, a0, a1, a2, a3, g, *rest[-6:])

    filled = () if before is None else (before,)
    return pl.pallas_call(
        kernel,
        grid_spec=pltpu.PrefetchScalarGridSpec(
            num_scalar_prefetch=1,
            grid=(1,),
            in_specs=[in_hbm()] * 4 + [same((tokens, width))] + [in_hbm()] * len(filled),
            out_specs=in_hbm(),
            scratch_shapes=[
                pltpu.VMEM((tokens, SEQS * width), BF16),
                pltpu.VMEM((4 * layers, tokens, block), BF16),
                pltpu.VMEM((SLOTS, block, width), F32),
                pltpu.SemaphoreType.DMA((SLOTS,)),
                pltpu.SemaphoreType.DMA((4 * layers,)),
            ],
        ),
        out_shape=shape,
        input_output_aliases={6: 0} if filled else {},
        compiler_params=pltpu.CompilerParams(vmem_limit_bytes=VMEM_LIMIT),
        cost_estimate=pl.CostEstimate(
            flops=8 * layers * block * width * tokens,
            transcendentals=0,
            bytes_accessed=16 * layers * block * width,
        ),
        name="final",
    )(place, *pieces, g, *filled)


def turn(value, axis, size, by):
    return lax.ppermute(value, axis, [(i, (i + by) % size) for i in range(size)])


def from_z(value, layers):
    return [value] + [turn(value, "z", layers, by) for by in range(1, layers)]


def in_order(pieces, z):
    layers = len(pieces)
    return jnp.stack([lax.select_n((z - i) % layers, *pieces) for i in range(layers)])


def over_chip(mine):
    across = turn(mine, "y", 2, 1)
    return mine, across, turn(mine, "core", 2, 1), turn(across, "core", 2, 1)


def pick(value, which):
    return lax.dynamic_index_in_dim(value, which, 0, keepdims=False)


def for_y(keep, got, y, layers):
    shape = (layers, 2) + keep.shape[1:]
    keep, got = keep.reshape(shape), got.reshape(shape)

    def total(which):
        return lax.dynamic_index_in_dim(keep, which, 1, keepdims=False) + (
            lax.dynamic_index_in_dim(got, which, 1, keepdims=False).astype(F32)
        )

    return total(1 - y).astype(BF16), total(y)


def for_z(keep, got, z, layers):
    total = keep + got.astype(F32)
    return [pick(total, (z + by) % layers).astype(BF16) for by in range(1, layers)], pick(total, z)


def reduce_z(sends, keep, layers):
    for by, send in enumerate(sends, 1):
        keep = keep + turn(send, "z", layers, by).astype(F32)
    return keep.astype(BF16)


def on_device(layers, activations, out_grad, loss_mask, w_gate, w_down, basis_a, basis_g):
    z, y, core = (lax.axis_index(name) for name in ("z", "y", "core"))
    chips = 2 * layers
    place = jnp.stack([z, y, core, lax.axis_index(("z", "y", "core"))]).astype(jnp.int32)
    masked = out_grad * loss_mask.astype(out_grad.dtype)[:, None]

    def flat(stacks):
        return [s.reshape(-1, s.shape[-1]) for s in stacks]

    act_z = in_order(from_z(activations, layers), z)
    grad_z = in_order(from_z(masked, layers), z)
    act = flat(over_chip(act_z))
    across = turn(grad_z, "y", 2, 1)
    send_a, keep_a = share_a(place, act, basis_a, chips, (grad_z,))
    gate, keep_a = gate_product(place, act, w_gate, (send_a,), (keep_a,))
    across = hold(place, across, gate)
    grad = flat((grad_z, across, turn(grad_z, "core", 2, 1), turn(across, "core", 2, 1)))
    send_a, keep_a = for_y(keep_a, turn(send_a, "core", 2, 1), y, layers)
    up, keep_a = down_product(place, grad, w_down, gate, (send_a,), (keep_a,))
    send_g, keep_a = share_g(place, up, basis_g, chips, 1, BF16, (send_a,), (keep_a,))
    sends_a, own_a = for_z(keep_a, turn(send_a, "y", 2, 1), z, layers)
    send_g = hold(place, send_g, sends_a[0])
    keep_g, own_a = share_g(place, up, basis_g, chips, 0, F32, (send_g,), (own_a,))
    send_g, keep_g = for_y(keep_g, turn(send_g, "core", 2, 1), y, layers)
    own_a = reduce_z(sends_a, hold(place, own_a, send_g), layers)
    pieces_a = from_z(own_a, layers)
    sends_g, own_g = for_z(keep_g, turn(send_g, "y", 2, 1), z, layers)
    pieces_a[0] = hold(place, own_a, sends_g[0])
    proj_a = over_chip(in_order(pieces_a, z))
    own_g = reduce_z(sends_g, own_g, layers)
    return final_product(place, proj_a, own_g, 0, own_g.shape[1], None)


def solution(mesh):
    tensor = mesh.shape["tensor"]
    chips = tensor // 2
    across = max(d for d in range(1, chips + 1) if chips % d == 0 and d * d <= chips)
    layers = chips // across
    fine = Mesh(
        mesh.devices.reshape(mesh.shape["parts"], layers, across, 2), ("parts", "z", "y", "core")
    )
    t = ("z", "y", "core")
    placed = (
        P(("parts",) + t, None),
        P(("parts",) + t, None),
        P(("parts",) + t),
        P(None, t),
        P(t, None),
        P(t, None),
        P(t, None),
    )

    def step(*args):
        rows = args[0].shape[0] // (mesh.shape["parts"] * tensor)
        small = across == 2 and layers * rows // SEQS == 16
        body = functools.partial(on_device, layers) if small else plain
        return jax.shard_map(
            body, mesh=fine, in_specs=placed, out_specs=P("parts", t), check_vma=False
        )(*args)

    return step
```

```python
import functools

import jax
import jax.numpy as jnp
from jax import lax
from jax.experimental import pallas as pl
from jax.experimental.pallas import tpu as pltpu
from jax.sharding import Mesh
from jax.sharding import PartitionSpec as P

SEQS = 2
F32 = jnp.float32
BF16 = jnp.bfloat16
VMEM_LIMIT = 52 * 1024 * 1024


def plain(activations, out_grad, loss_mask, w_gate, w_down, basis_a, basis_g):
    axes = ("z", "y", "core")
    masked = out_grad * loss_mask.astype(out_grad.dtype)[:, None]
    whole_act = lax.all_gather(activations, axes, axis=0, tiled=True)
    whole_grad = lax.all_gather(masked, axes, axis=0, tiled=True)
    gate_pre = jnp.dot(whole_act, w_gate, preferred_element_type=F32)
    hid_grad = lax.dot_general(
        whole_grad, w_down, (((1,), (1,)), ((), ())), preferred_element_type=F32
    )
    up_grad = (hid_grad * jax.nn.silu(gate_pre)).astype(BF16)
    depth = basis_a.shape[0]
    own_act = lax.dynamic_slice_in_dim(whole_act, lax.axis_index(axes) * depth, depth, axis=1)
    share_a = lax.psum_scatter(
        jnp.dot(own_act, basis_a, preferred_element_type=F32),
        axes,
        scatter_dimension=1,
        tiled=True,
    ).astype(BF16)
    proj_a = lax.all_gather(share_a, axes, axis=1, tiled=True)
    proj_g_cols = lax.psum_scatter(
        lax.dot_general(basis_g, up_grad, (((0,), (1,)), ((), ())), preferred_element_type=F32),
        axes,
        scatter_dimension=0,
        tiled=True,
    ).astype(BF16)
    tokens = proj_a.shape[0]
    seq = tokens // SEQS
    total = 0.0
    for which in range(SEQS):
        rows = slice(which * seq, (which + 1) * seq)
        product = lax.dot_general(
            proj_a[rows],
            proj_g_cols[:, rows],
            (((0,), (1,)), ((), ())),
            preferred_element_type=F32,
        )
        total = total + product * product
    return total / tokens


def in_hbm():
    return pl.BlockSpec(memory_space=pltpu.HBM)


def anywhere():
    return pl.BlockSpec(memory_space=pl.ANY)


def same(shape):
    return pl.BlockSpec(shape, lambda i, s: (0,) * len(shape))


def call(kernel, place, operands, in_specs, outs, out_specs, scratch, flops, moved, name, after=(), through=()):
    n_in, n_out, n_after, n_through = len(operands), len(outs), len(after), len(through)
    skip = n_in + n_after + n_through

    def body(place, *refs):
        rest = refs[skip : skip + n_out] + refs[skip + n_out + n_through :]
        kernel(place, *refs[:n_in], *rest)

    return pl.pallas_call(
        body,
        grid_spec=pltpu.PrefetchScalarGridSpec(
            num_scalar_prefetch=1,
            grid=(1,),
            in_specs=list(in_specs) + [anywhere()] * (n_after + n_through),
            out_specs=list(out_specs) + [anywhere()] * n_through,
            scratch_shapes=scratch,
        ),
        out_shape=list(outs) + [jax.ShapeDtypeStruct(t.shape, t.dtype) for t in through],
        input_output_aliases={1 + n_in + n_after + i: n_out + i for i in range(n_through)},
        compiler_params=pltpu.CompilerParams(vmem_limit_bytes=VMEM_LIMIT),
        cost_estimate=pl.CostEstimate(flops=flops, transcendentals=0, bytes_accessed=moved),
        name=name,
    )(place, *operands, *after, *through)


def hold(place, value, *after):
    return call(lambda place: None, place, (), [], [], [], [], 0, 0, "hold", after, (value,))[0]


def row_copies(place, pieces, start_column, columns, whole, sems):
    part = pieces[0].shape[0] // SEQS
    copies = []
    for other in range(2):
        for across in range(2):
            core = (place[2] + other) % 2
            y = (place[1] + across) % 2
            for which in range(SEQS):
                start = pl.multiple_of(((which * 2 + core) * 2 + y) * part, part)
                copies.append(
                    pltpu.make_async_copy(
                        pieces[other * 2 + across].at[
                            pl.ds(which * part, part), pl.ds(start_column, columns)
                        ],
                        whole.at[pl.ds(start, part), :],
                        sems.at[len(copies)],
                    )
                )
    return copies


def start_all(copies):
    for copy in copies:
        copy.start()


def wait_all(copies):
    for copy in copies:
        copy.wait()


def down_kernel(steps, place, p0, p1, p2, p3, weight, gate, out, whole, buffer, sems, row_sems):
    rows_in = row_copies(place, (p0, p1, p2, p3), 0, whole.shape[1], whole, row_sems)
    start_all(rows_in)
    depth = weight.shape[1] // steps
    copies = []
    for i in range(steps):
        columns = pl.ds(i * depth, depth)
        copies.append(pltpu.make_async_copy(weight.at[:, columns], buffer.at[:, columns], sems.at[i]))
    start_all(copies)
    wait_all(rows_in)
    total = None
    for i in range(steps):
        copies[i].wait()
        part = slice(i * depth, (i + 1) * depth)
        product = lax.dot_general(
            whole[:, part], buffer[:, part], (((1,), (1,)), ((), ())), preferred_element_type=F32
        )
        total = product if total is None else total + product
    pre = gate[...]
    out[...] = (total * (pre / (1.0 + jnp.exp(-pre)))).astype(out.dtype)


def down_product(place, pieces, weight, gate, after, through, steps=8):
    rows, depth = pieces[0].shape
    width = weight.shape[0]
    return call(
        functools.partial(down_kernel, steps),
        place,
        (*pieces, weight, gate),
        [in_hbm()] * 5 + [same((4 * rows, width))],
        [jax.ShapeDtypeStruct((4 * rows, width), BF16)],
        [same((4 * rows, width))],
        [
            pltpu.VMEM((4 * rows, depth), BF16),
            pltpu.VMEM((width, depth), BF16),
            pltpu.SemaphoreType.DMA((steps,)),
            pltpu.SemaphoreType.DMA((4 * SEQS,)),
        ],
        8 * rows * depth * width,
        2 * depth * width,
        "down",
        after=after,
        through=through,
    )


def share_copies(place, basis, flip, block, buffer, sems):
    copies = []
    for chip in range(buffer.shape[0]):
        start = pl.multiple_of((2 * chip + (place[2] + flip) % 2) * block, block)
        copies.append(
            pltpu.make_async_copy(basis.at[:, pl.ds(start, block)], buffer.at[chip], sems.at[chip])
        )
    return copies


def share_products(left, copies, buffer, out):
    for chip, copy in enumerate(copies):
        copy.wait()
        out[chip] = jnp.dot(left[...], buffer[chip], preferred_element_type=F32).astype(out.dtype)


def front_kernel(steps, block, place, p0, p1, p2, p3, weight, basis, gate, send, keep, whole, left, buffer, buf0, buf1, sems, row_sems, left_sems, share_sems):
    pieces = (p0, p1, p2, p3)
    depth_a = left.shape[1]
    start = pl.multiple_of(place[3] * depth_a, depth_a)
    rows_in = row_copies(place, pieces, start, depth_a, left, left_sems)
    whole_in = row_copies(place, pieces, 0, whole.shape[1], whole, row_sems)
    sent = share_copies(place, basis, 1, block, buf0, share_sems.at[0])
    kept = share_copies(place, basis, 0, block, buf1, share_sems.at[1])
    depth = weight.shape[0] // steps
    copies = []
    for i in range(steps):
        rows = pl.ds(i * depth, depth)
        copies.append(pltpu.make_async_copy(weight.at[rows], buffer.at[rows], sems.at[i]))
    for some in (rows_in, sent, kept, whole_in, copies):
        start_all(some)
    wait_all(rows_in)
    share_products(left, sent, buf0, send)
    share_products(left, kept, buf1, keep)
    wait_all(whole_in)
    total = None
    for i in range(steps):
        copies[i].wait()
        part = slice(i * depth, (i + 1) * depth)
        product = jnp.dot(whole[:, part], buffer[part, :], preferred_element_type=F32)
        total = product if total is None else total + product
    gate[...] = total


def front(place, pieces, weight, basis, chips, after, steps=8):
    rows, depth = pieces[0].shape
    width = weight.shape[1]
    depth_a, columns = basis.shape
    block = columns // (2 * chips)
    shape = (chips, 4 * rows, block)
    return call(
        functools.partial(front_kernel, steps, block),
        place,
        (*pieces, weight, basis),
        [in_hbm()] * 6,
        [
            jax.ShapeDtypeStruct((4 * rows, width), F32),
            jax.ShapeDtypeStruct(shape, BF16),
            jax.ShapeDtypeStruct(shape, F32),
        ],
        [same((4 * rows, width)), same(shape), same(shape)],
        [
            pltpu.VMEM((4 * rows, depth), BF16),
            pltpu.VMEM((4 * rows, depth_a), BF16),
            pltpu.VMEM((depth, width), BF16),
            pltpu.VMEM((chips, depth_a, block), BF16),
            pltpu.VMEM((chips, depth_a, block), BF16),
            pltpu.SemaphoreType.DMA((steps,)),
            pltpu.SemaphoreType.DMA((4 * SEQS,)),
            pltpu.SemaphoreType.DMA((4 * SEQS,)),
            pltpu.SemaphoreType.DMA((2, chips)),
        ],
        8 * rows * (depth * width + depth_a * columns),
        2 * (depth * width + depth_a * columns),
        "front",
        after=after,
    )


def share_g_kernel(block, place, up, basis, send, keep, buf0, buf1, sems):
    sent = share_copies(place, basis, 1, block, buf0, sems.at[0])
    kept = share_copies(place, basis, 0, block, buf1, sems.at[1])
    start_all(sent)
    start_all(kept)
    share_products(up, sent, buf0, send)
    share_products(up, kept, buf1, keep)


def share_g(place, up, basis, chips, after, through):
    tokens, depth = up.shape
    block = basis.shape[1] // (2 * chips)
    shape = (chips, tokens, block)
    return call(
        functools.partial(share_g_kernel, block),
        place,
        (up, basis),
        [same((tokens, depth)), in_hbm()],
        [jax.ShapeDtypeStruct(shape, BF16), jax.ShapeDtypeStruct(shape, F32)],
        [same(shape), same(shape)],
        [pltpu.VMEM((chips, depth, block), BF16)] * 2 + [pltpu.SemaphoreType.DMA((2, chips))],
        4 * tokens * depth * chips * block,
        4 * depth * chips * block,
        "share_g",
        after=after,
        through=through,
    )


SLOTS = 8


def final_kernel(layers, first, place, a0, a1, a2, a3, g, out, pair, left, stage, sems, in_sems):
    pieces = (a0, a1, a2, a3)
    tokens, width = g.shape
    seq = tokens // SEQS
    block = stage.shape[1]
    loads = [
        pltpu.make_async_copy(pieces[which].at[z], left.at[which * layers + z], in_sems.at[which * layers + z])
        for which in range(4)
        for z in range(layers)
    ]
    start_all(loads)
    pair[...] = jnp.zeros_like(pair)
    for s in range(SEQS):
        rows = slice(s * seq, (s + 1) * seq)
        pair[rows, s * width : (s + 1) * width] = g[rows, :]
    copies = []
    for step in range(4 * layers):
        which, z = divmod(step, layers)
        core = (place[2] + which // 2) % 2
        y = (place[1] + which) % 2
        slot = step % SLOTS
        loads[step].wait()
        if step >= SLOTS:
            copies[step - SLOTS].wait()
        product = lax.dot_general(
            left[step], pair[...], (((0,), (0,)), ((), ())), preferred_element_type=F32
        )
        total = None
        for s in range(SEQS):
            one = product[:, s * width : (s + 1) * width]
            total = one * one if total is None else total + one * one
        stage[slot] = total * (1.0 / tokens)
        start = pl.multiple_of(((z * 2 + y) * 2 + core) * block, block)
        copies.append(
            pltpu.make_async_copy(
                stage.at[slot],
                out.at[pl.ds(start, block), pl.ds(first, width)],
                sems.at[slot],
            )
        )
        copies[step].start()
    wait_all(copies[-SLOTS:])


def final_product(place, pieces, g, first, columns, before):
    layers, tokens, block = pieces[0].shape
    width = g.shape[1]
    shape = jax.ShapeDtypeStruct((4 * layers * block, columns), F32)

    def kernel(place, a0, a1, a2, a3, g, *rest):
        final_kernel(layers, first, place, a0, a1, a2, a3, g, *rest[-6:])

    filled = () if before is None else (before,)
    return pl.pallas_call(
        kernel,
        grid_spec=pltpu.PrefetchScalarGridSpec(
            num_scalar_prefetch=1,
            grid=(1,),
            in_specs=[in_hbm()] * 4 + [same((tokens, width))] + [in_hbm()] * len(filled),
            out_specs=in_hbm(),
            scratch_shapes=[
                pltpu.VMEM((tokens, SEQS * width), BF16),
                pltpu.VMEM((4 * layers, tokens, block), BF16),
                pltpu.VMEM((SLOTS, block, width), F32),
                pltpu.SemaphoreType.DMA((SLOTS,)),
                pltpu.SemaphoreType.DMA((4 * layers,)),
            ],
        ),
        out_shape=shape,
        input_output_aliases={6: 0} if filled else {},
        compiler_params=pltpu.CompilerParams(vmem_limit_bytes=VMEM_LIMIT),
        cost_estimate=pl.CostEstimate(
            flops=8 * layers * block * width * tokens,
            transcendentals=0,
            bytes_accessed=16 * layers * block * width,
        ),
        name="final",
    )(place, *pieces, g, *filled)


def turn(value, axis, size, by):
    return lax.ppermute(value, axis, [(i, (i + by) % size) for i in range(size)])


def from_z(value, layers):
    return [value] + [turn(value, "z", layers, by) for by in range(1, layers)]


def in_order(pieces, z):
    layers = len(pieces)
    return jnp.stack([lax.select_n((z - i) % layers, *pieces) for i in range(layers)])


def over_chip(mine):
    across = turn(mine, "y", 2, 1)
    return mine, across, turn(mine, "core", 2, 1), turn(across, "core", 2, 1)


def pick(value, which):
    return lax.dynamic_index_in_dim(value, which, 0, keepdims=False)


def for_y(keep, got, y, layers):
    shape = (layers, 2) + keep.shape[1:]
    keep, got = keep.reshape(shape), got.reshape(shape)

    def total(which):
        return lax.dynamic_index_in_dim(keep, which, 1, keepdims=False) + (
            lax.dynamic_index_in_dim(got, which, 1, keepdims=False).astype(F32)
        )

    return total(1 - y).astype(BF16), total(y)


def for_z(keep, got, z, layers):
    total = keep + got.astype(F32)
    return [pick(total, (z + by) % layers).astype(BF16) for by in range(1, layers)], pick(total, z)


def from_others(sends, layers):
    return [turn(send, "z", layers, by) for by, send in enumerate(sends, 1)]


def summed(keep, got):
    for one in got:
        keep = keep + one.astype(F32)
    return keep.astype(BF16)


def on_device(layers, activations, out_grad, loss_mask, w_gate, w_down, basis_a, basis_g):
    z, y, core = (lax.axis_index(name) for name in ("z", "y", "core"))
    chips = 2 * layers
    place = jnp.stack([z, y, core, lax.axis_index(("z", "y", "core"))]).astype(jnp.int32)
    masked = out_grad * loss_mask.astype(out_grad.dtype)[:, None]

    def flat(stacks):
        return [s.reshape(-1, s.shape[-1]) for s in stacks]

    act_z = in_order(from_z(activations, layers), z)
    grad_z = in_order(from_z(masked, layers), z)
    act = flat(over_chip(act_z))
    across = turn(grad_z, "y", 2, 1)
    gate, send_a, keep_a = front(place, act, w_gate, basis_a, chips, (grad_z,))
    across = hold(place, across, gate)
    send_a = hold(place, send_a, across)
    grad = flat((grad_z, across, turn(grad_z, "core", 2, 1), turn(across, "core", 2, 1)))
    send_a, keep_a = for_y(keep_a, turn(send_a, "core", 2, 1), y, layers)
    up, keep_a = down_product(place, grad, w_down, gate, (send_a,), (keep_a,))
    sends_a, own_a = for_z(keep_a, turn(send_a, "y", 2, 1), z, layers)
    send_g, keep_g, own_a = share_g(place, up, basis_g, chips, (sends_a[0],), (own_a,))
    own_a = summed(own_a, from_others(sends_a, layers))
    send_g = hold(place, send_g, own_a)
    send_g, keep_g = for_y(keep_g, turn(send_g, "core", 2, 1), y, layers)
    pieces_a = from_z(own_a, layers)
    sends_g, own_g = for_z(keep_g, turn(send_g, "y", 2, 1), z, layers)
    own_g = summed(own_g, from_others(sends_g, layers))
    pieces_a[0] = hold(place, own_a, sends_g[0])
    mine = in_order(pieces_a, z)
    across = hold(place, turn(mine, "y", 2, 1), own_g)
    proj_a = mine, across, turn(mine, "core", 2, 1), turn(across, "core", 2, 1)
    return final_product(place, proj_a, own_g, 0, own_g.shape[1], None)


def solution(mesh):
    tensor = mesh.shape["tensor"]
    chips = tensor // 2
    across = max(d for d in range(1, chips + 1) if chips % d == 0 and d * d <= chips)
    layers = chips // across
    fine = Mesh(
        mesh.devices.reshape(mesh.shape["parts"], layers, across, 2), ("parts", "z", "y", "core")
    )
    t = ("z", "y", "core")
    placed = (
        P(("parts",) + t, None),
        P(("parts",) + t, None),
        P(("parts",) + t),
        P(None, t),
        P(t, None),
        P(t, None),
        P(t, None),
    )

    def step(*args):
        rows = args[0].shape[0] // (mesh.shape["parts"] * tensor)
        small = across == 2 and layers * rows // SEQS == 16
        body = functools.partial(on_device, layers) if small else plain
        return jax.shard_map(
            body, mesh=fine, in_specs=placed, out_specs=P("parts", t), check_vma=False
        )(*args)

    return step
```

```python
import functools

import jax
import jax.numpy as jnp
from jax import lax
from jax.experimental import pallas as pl
from jax.experimental.pallas import tpu as pltpu
from jax.sharding import Mesh
from jax.sharding import PartitionSpec as P

SEQS = 2
F32 = jnp.float32
BF16 = jnp.bfloat16
MIB = 1024 * 1024


def plain(activations, out_grad, loss_mask, w_gate, w_down, basis_a, basis_g):
    axes = ("z", "y", "core")
    masked = out_grad * loss_mask.astype(out_grad.dtype)[:, None]
    whole_act = lax.all_gather(activations, axes, axis=0, tiled=True)
    whole_grad = lax.all_gather(masked, axes, axis=0, tiled=True)
    gate_pre = jnp.dot(whole_act, w_gate, preferred_element_type=F32)
    hid_grad = lax.dot_general(
        whole_grad, w_down, (((1,), (1,)), ((), ())), preferred_element_type=F32
    )
    up_grad = (hid_grad * jax.nn.silu(gate_pre)).astype(BF16)
    depth = basis_a.shape[0]
    own_act = lax.dynamic_slice_in_dim(whole_act, lax.axis_index(axes) * depth, depth, axis=1)
    share_a = lax.psum_scatter(
        jnp.dot(own_act, basis_a, preferred_element_type=F32),
        axes,
        scatter_dimension=1,
        tiled=True,
    ).astype(BF16)
    proj_a = lax.all_gather(share_a, axes, axis=1, tiled=True)
    proj_g_cols = lax.psum_scatter(
        lax.dot_general(basis_g, up_grad, (((0,), (1,)), ((), ())), preferred_element_type=F32),
        axes,
        scatter_dimension=0,
        tiled=True,
    ).astype(BF16)
    tokens = proj_a.shape[0]
    seq = tokens // SEQS
    total = 0.0
    for which in range(SEQS):
        rows = slice(which * seq, (which + 1) * seq)
        product = lax.dot_general(
            proj_a[rows],
            proj_g_cols[:, rows],
            (((0,), (1,)), ((), ())),
            preferred_element_type=F32,
        )
        total = total + product * product
    return total / tokens


def in_hbm():
    return pl.BlockSpec(memory_space=pltpu.HBM)


def anywhere():
    return pl.BlockSpec(memory_space=pl.ANY)


def same(shape):
    return pl.BlockSpec(shape, lambda i, s: (0,) * len(shape))


def call(kernel, place, operands, in_specs, outs, out_specs, scratch, flops, moved, name, after=(), through=(), limit=52):
    n_in, n_out, n_after, n_through = len(operands), len(outs), len(after), len(through)
    skip = n_in + n_after + n_through

    def body(place, *refs):
        rest = refs[skip : skip + n_out] + refs[skip + n_out + n_through :]
        kernel(place, *refs[:n_in], *rest)

    return pl.pallas_call(
        body,
        grid_spec=pltpu.PrefetchScalarGridSpec(
            num_scalar_prefetch=1,
            grid=(1,),
            in_specs=list(in_specs) + [anywhere()] * (n_after + n_through),
            out_specs=list(out_specs) + [anywhere()] * n_through,
            scratch_shapes=scratch,
        ),
        out_shape=list(outs) + [jax.ShapeDtypeStruct(t.shape, t.dtype) for t in through],
        input_output_aliases={1 + n_in + n_after + i: n_out + i for i in range(n_through)},
        compiler_params=pltpu.CompilerParams(vmem_limit_bytes=limit * MIB),
        cost_estimate=pl.CostEstimate(flops=flops, transcendentals=0, bytes_accessed=moved),
        name=name,
    )(place, *operands, *after, *through)


def hold(value, *after):
    return pl.pallas_call(
        lambda *refs: None,
        in_specs=[anywhere()] * (1 + len(after)),
        out_specs=anywhere(),
        out_shape=jax.ShapeDtypeStruct(value.shape, value.dtype),
        input_output_aliases={0: 0},
        compiler_params=pltpu.CompilerParams(vmem_limit_bytes=MIB),
        name="hold",
    )(value, *after)


def row_copies(place, pieces, start_column, columns, whole, sems):
    part = pieces[0].shape[0] // SEQS
    copies = []
    for other in range(2):
        for across in range(2):
            core = (place[2] + other) % 2
            y = (place[1] + across) % 2
            for which in range(SEQS):
                start = pl.multiple_of(((which * 2 + core) * 2 + y) * part, part)
                copies.append(
                    pltpu.make_async_copy(
                        pieces[other * 2 + across].at[
                            pl.ds(which * part, part), pl.ds(start_column, columns)
                        ],
                        whole.at[pl.ds(start, part), :],
                        sems.at[len(copies)],
                    )
                )
    return copies


def start_all(copies):
    for copy in copies:
        copy.start()


def wait_all(copies):
    for copy in copies:
        copy.wait()


def down_kernel(steps, place, p0, p1, p2, p3, weight, gate, out, whole, buffer, sems, row_sems):
    rows_in = row_copies(place, (p0, p1, p2, p3), 0, whole.shape[1], whole, row_sems)
    start_all(rows_in)
    depth = weight.shape[1] // steps
    copies = []
    for i in range(steps):
        columns = pl.ds(i * depth, depth)
        copies.append(pltpu.make_async_copy(weight.at[:, columns], buffer.at[:, columns], sems.at[i]))
    start_all(copies)
    wait_all(rows_in)
    total = None
    for i in range(steps):
        copies[i].wait()
        part = slice(i * depth, (i + 1) * depth)
        product = lax.dot_general(
            whole[:, part], buffer[:, part], (((1,), (1,)), ((), ())), preferred_element_type=F32
        )
        total = product if total is None else total + product
    pre = gate[...]
    out[...] = (total * (pre / (1.0 + jnp.exp(-pre)))).astype(out.dtype)


def down_product(place, pieces, weight, gate, after, through, steps=4):
    rows, depth = pieces[0].shape
    width = weight.shape[0]
    return call(
        functools.partial(down_kernel, steps),
        place,
        (*pieces, weight, gate),
        [in_hbm()] * 5 + [pl.BlockSpec(memory_space=pltpu.VMEM)],
        [jax.ShapeDtypeStruct((4 * rows, width), BF16)],
        [same((4 * rows, width))],
        [
            pltpu.VMEM((4 * rows, depth), BF16),
            pltpu.VMEM((width, depth), BF16),
            pltpu.SemaphoreType.DMA((steps,)),
            pltpu.SemaphoreType.DMA((4 * SEQS,)),
        ],
        8 * rows * depth * width,
        2 * depth * width,
        "down",
        after=after,
        through=through,
    )


def share_copies(place, basis, flip, block, buffer, sems):
    copies = []
    for chip in range(buffer.shape[0]):
        start = pl.multiple_of((2 * chip + (place[2] + flip) % 2) * block, block)
        copies.append(
            pltpu.make_async_copy(basis.at[:, pl.ds(start, block)], buffer.at[chip], sems.at[chip])
        )
    return copies


def share_products(left, copies, buffer, out):
    for chip, copy in enumerate(copies):
        copy.wait()
        out[chip] = jnp.dot(left[...], buffer[chip], preferred_element_type=F32).astype(out.dtype)


def front_kernel(steps, block, place, p0, p1, p2, p3, weight, basis, gate, send, keep, whole, left, buffer, buf0, buf1, sems, row_sems, left_sems, share_sems):
    pieces = (p0, p1, p2, p3)
    depth_a = left.shape[1]
    start = pl.multiple_of(place[3] * depth_a, depth_a)
    rows_in = row_copies(place, pieces, start, depth_a, left, left_sems)
    whole_in = row_copies(place, pieces, 0, whole.shape[1], whole, row_sems)
    sent = share_copies(place, basis, 1, block, buf0, share_sems.at[0])
    kept = share_copies(place, basis, 0, block, buf1, share_sems.at[1])
    depth = weight.shape[0] // steps
    copies = []
    for i in range(steps):
        rows = pl.ds(i * depth, depth)
        copies.append(pltpu.make_async_copy(weight.at[rows], buffer.at[rows], sems.at[i]))
    for some in (rows_in, sent, kept, whole_in, copies):
        start_all(some)
    wait_all(rows_in)
    share_products(left, sent, buf0, send)
    share_products(left, kept, buf1, keep)
    wait_all(whole_in)
    total = None
    for i in range(steps):
        copies[i].wait()
        part = slice(i * depth, (i + 1) * depth)
        product = jnp.dot(whole[:, part], buffer[part, :], preferred_element_type=F32)
        total = product if total is None else total + product
    gate[...] = total


def front(place, pieces, weight, basis, chips, after, steps=8):
    rows, depth = pieces[0].shape
    width = weight.shape[1]
    depth_a, columns = basis.shape
    block = columns // (2 * chips)
    shape = (chips, 4 * rows, block)
    return call(
        functools.partial(front_kernel, steps, block),
        place,
        (*pieces, weight, basis),
        [in_hbm()] * 6,
        [
            jax.ShapeDtypeStruct((4 * rows, width), F32),
            jax.ShapeDtypeStruct(shape, BF16),
            jax.ShapeDtypeStruct(shape, F32),
        ],
        [same((4 * rows, width)), same(shape), same(shape)],
        [
            pltpu.VMEM((4 * rows, depth), BF16),
            pltpu.VMEM((4 * rows, depth_a), BF16),
            pltpu.VMEM((depth, width), BF16),
            pltpu.VMEM((chips, depth_a, block), BF16),
            pltpu.VMEM((chips, depth_a, block), BF16),
            pltpu.SemaphoreType.DMA((steps,)),
            pltpu.SemaphoreType.DMA((4 * SEQS,)),
            pltpu.SemaphoreType.DMA((4 * SEQS,)),
            pltpu.SemaphoreType.DMA((2, chips)),
        ],
        8 * rows * (depth * width + depth_a * columns),
        2 * (depth * width + depth_a * columns),
        "front",
        after=after,
    )


def share_g_kernel(block, place, up, basis, send, keep, buf0, buf1, sems):
    sent = share_copies(place, basis, 1, block, buf0, sems.at[0])
    kept = share_copies(place, basis, 0, block, buf1, sems.at[1])
    start_all(sent)
    start_all(kept)
    share_products(up, sent, buf0, send)
    share_products(up, kept, buf1, keep)


def share_g(place, up, basis, chips, after, through):
    tokens, depth = up.shape
    block = basis.shape[1] // (2 * chips)
    shape = (chips, tokens, block)
    return call(
        functools.partial(share_g_kernel, block),
        place,
        (up, basis),
        [pl.BlockSpec(memory_space=pltpu.VMEM), in_hbm()],
        [jax.ShapeDtypeStruct(shape, BF16), jax.ShapeDtypeStruct(shape, F32)],
        [same(shape), same(shape)],
        [pltpu.VMEM((chips, depth, block), BF16)] * 2 + [pltpu.SemaphoreType.DMA((2, chips))],
        4 * tokens * depth * chips * block,
        4 * depth * chips * block,
        "share_g",
        after=after,
        through=through,
        limit=40,
    )


SLOTS = 8


def final_kernel(layers, place, a0, a1, a2, a3, g, out, pair, stage, sems):
    tokens, width = g.shape
    seq = tokens // SEQS
    block = stage.shape[1]
    pair[...] = jnp.zeros_like(pair)
    for s in range(SEQS):
        rows = slice(s * seq, (s + 1) * seq)
        pair[rows, s * width : (s + 1) * width] = g[rows, :]
    copies = []
    for step in range(4 * layers):
        which, z = divmod(step, layers)
        core = (place[2] + which // 2) % 2
        y = (place[1] + which) % 2
        slot = step % SLOTS
        if step >= SLOTS:
            copies[step - SLOTS].wait()
        product = lax.dot_general(
            (a0, a1, a2, a3)[which][z],
            pair[...],
            (((0,), (0,)), ((), ())),
            preferred_element_type=F32,
        )
        total = None
        for s in range(SEQS):
            one = product[:, s * width : (s + 1) * width]
            total = one * one if total is None else total + one * one
        stage[slot] = total * (1.0 / tokens)
        start = pl.multiple_of(((z * 2 + y) * 2 + core) * block, block)
        copies.append(
            pltpu.make_async_copy(stage.at[slot], out.at[pl.ds(start, block)], sems.at[slot])
        )
        copies[step].start()
    wait_all(copies[-SLOTS:])


def final_product(place, pieces, g):
    layers, tokens, block = pieces[0].shape
    width = g.shape[1]
    return call(
        functools.partial(final_kernel, layers),
        place,
        (*pieces, g),
        [pl.BlockSpec(memory_space=pltpu.VMEM)] * 5,
        [jax.ShapeDtypeStruct((4 * layers * block, width), F32)],
        [in_hbm()],
        [
            pltpu.VMEM((tokens, SEQS * width), BF16),
            pltpu.VMEM((SLOTS, block, width), F32),
            pltpu.SemaphoreType.DMA((SLOTS,)),
        ],
        8 * layers * block * width * tokens,
        16 * layers * block * width,
        "final",
        limit=24,
    )[0]


def turn(value, axis, size, by):
    return lax.ppermute(value, axis, [(i, (i + by) % size) for i in range(size)])


def from_z(value, layers):
    return [value] + [turn(value, "z", layers, by) for by in range(1, layers)]


def in_order(pieces, z):
    layers = len(pieces)
    return jnp.stack([lax.select_n((z - i) % layers, *pieces) for i in range(layers)])


def over_chip(mine):
    across = turn(mine, "y", 2, 1)
    return mine, across, turn(mine, "core", 2, 1), turn(across, "core", 2, 1)


def pick(value, which):
    return lax.dynamic_index_in_dim(value, which, 0, keepdims=False)


def for_y(keep, got, y, layers):
    shape = (layers, 2) + keep.shape[1:]
    keep, got = keep.reshape(shape), got.reshape(shape)

    def total(which):
        return lax.dynamic_index_in_dim(keep, which, 1, keepdims=False) + (
            lax.dynamic_index_in_dim(got, which, 1, keepdims=False).astype(F32)
        )

    return total(1 - y).astype(BF16), total(y)


def for_z(keep, got, z, layers):
    total = keep + got.astype(F32)
    return [pick(total, (z + by) % layers).astype(BF16) for by in range(1, layers)], pick(total, z)


def from_others(sends, layers):
    return [turn(send, "z", layers, by) for by, send in enumerate(sends, 1)]


def summed(keep, got):
    for one in got:
        keep = keep + one.astype(F32)
    return keep.astype(BF16)


def on_device(layers, activations, out_grad, loss_mask, w_gate, w_down, basis_a, basis_g):
    z, y, core = (lax.axis_index(name) for name in ("z", "y", "core"))
    chips = 2 * layers
    place = jnp.stack([z, y, core, lax.axis_index(("z", "y", "core"))]).astype(jnp.int32)
    masked = out_grad * loss_mask.astype(out_grad.dtype)[:, None]

    def flat(stacks):
        return [s.reshape(-1, s.shape[-1]) for s in stacks]

    act_z = in_order(from_z(activations, layers), z)
    grad_z = in_order(from_z(masked, layers), z)
    act = flat(over_chip(act_z))
    across = turn(grad_z, "y", 2, 1)
    gate, send_a, keep_a = front(place, act, w_gate, basis_a, chips, (grad_z,))
    across = hold(across, gate)
    send_a = hold(send_a, across)
    grad = flat((grad_z, across, turn(grad_z, "core", 2, 1), turn(across, "core", 2, 1)))
    send_a, keep_a = for_y(keep_a, turn(send_a, "core", 2, 1), y, layers)
    up, keep_a = down_product(place, grad, w_down, gate, (send_a,), (keep_a,))
    sends_a, own_a = for_z(keep_a, turn(send_a, "y", 2, 1), z, layers)
    send_g, keep_g, own_a = share_g(place, up, basis_g, chips, (sends_a[0],), (own_a,))
    own_a = summed(own_a, from_others(sends_a, layers))
    send_g = hold(send_g, own_a)
    send_g, keep_g = for_y(keep_g, turn(send_g, "core", 2, 1), y, layers)
    pieces_a = from_z(own_a, layers)
    sends_g, own_g = for_z(keep_g, turn(send_g, "y", 2, 1), z, layers)
    own_g = summed(own_g, from_others(sends_g, layers))
    pieces_a[0] = hold(own_a, sends_g[0])
    mine = in_order(pieces_a, z)
    across = hold(turn(mine, "y", 2, 1), own_g)
    proj_a = mine, across, turn(mine, "core", 2, 1), turn(across, "core", 2, 1)
    return final_product(place, proj_a, own_g)


def solution(mesh):
    tensor = mesh.shape["tensor"]
    chips = tensor // 2
    across = max(d for d in range(1, chips + 1) if chips % d == 0 and d * d <= chips)
    layers = chips // across
    fine = Mesh(
        mesh.devices.reshape(mesh.shape["parts"], layers, across, 2), ("parts", "z", "y", "core")
    )
    t = ("z", "y", "core")
    placed = (
        P(("parts",) + t, None),
        P(("parts",) + t, None),
        P(("parts",) + t),
        P(None, t),
        P(t, None),
        P(t, None),
        P(t, None),
    )

    def step(*args):
        rows = args[0].shape[0] // (mesh.shape["parts"] * tensor)
        small = across == 2 and layers * rows // SEQS == 16
        body = functools.partial(on_device, layers) if small else plain
        return jax.shard_map(
            body, mesh=fine, in_specs=placed, out_specs=P("parts", t), check_vma=False
        )(*args)

    return step
```

```python
import functools

import jax
import jax.numpy as jnp
from jax import lax
from jax.experimental import pallas as pl
from jax.experimental.pallas import tpu as pltpu
from jax.sharding import Mesh
from jax.sharding import PartitionSpec as P

SEQS = 2
F32 = jnp.float32
BF16 = jnp.bfloat16
MIB = 1024 * 1024


def plain(activations, out_grad, loss_mask, w_gate, w_down, basis_a, basis_g):
    axes = ("z", "y", "core")
    masked = out_grad * loss_mask.astype(out_grad.dtype)[:, None]
    whole_act = lax.all_gather(activations, axes, axis=0, tiled=True)
    whole_grad = lax.all_gather(masked, axes, axis=0, tiled=True)
    gate_pre = jnp.dot(whole_act, w_gate, preferred_element_type=F32)
    hid_grad = lax.dot_general(
        whole_grad, w_down, (((1,), (1,)), ((), ())), preferred_element_type=F32
    )
    up_grad = (hid_grad * jax.nn.silu(gate_pre)).astype(BF16)
    depth = basis_a.shape[0]
    own_act = lax.dynamic_slice_in_dim(whole_act, lax.axis_index(axes) * depth, depth, axis=1)
    share_a = lax.psum_scatter(
        jnp.dot(own_act, basis_a, preferred_element_type=F32),
        axes,
        scatter_dimension=1,
        tiled=True,
    ).astype(BF16)
    proj_a = lax.all_gather(share_a, axes, axis=1, tiled=True)
    proj_g_cols = lax.psum_scatter(
        lax.dot_general(basis_g, up_grad, (((0,), (1,)), ((), ())), preferred_element_type=F32),
        axes,
        scatter_dimension=0,
        tiled=True,
    ).astype(BF16)
    tokens = proj_a.shape[0]
    seq = tokens // SEQS
    total = 0.0
    for which in range(SEQS):
        rows = slice(which * seq, (which + 1) * seq)
        product = lax.dot_general(
            proj_a[rows],
            proj_g_cols[:, rows],
            (((0,), (1,)), ((), ())),
            preferred_element_type=F32,
        )
        total = total + product * product
    return total / tokens


def in_hbm():
    return pl.BlockSpec(memory_space=pltpu.HBM)


def anywhere():
    return pl.BlockSpec(memory_space=pl.ANY)


def same(shape):
    return pl.BlockSpec(shape, lambda i, s: (0,) * len(shape))


def call(kernel, place, operands, in_specs, outs, out_specs, scratch, flops, moved, name, after=(), through=(), limit=52):
    n_in, n_out, n_after, n_through = len(operands), len(outs), len(after), len(through)
    skip = n_in + n_after + n_through

    def body(place, *refs):
        rest = refs[skip : skip + n_out] + refs[skip + n_out + n_through :]
        kernel(place, *refs[:n_in], *rest)

    return pl.pallas_call(
        body,
        grid_spec=pltpu.PrefetchScalarGridSpec(
            num_scalar_prefetch=1,
            grid=(1,),
            in_specs=list(in_specs) + [anywhere()] * (n_after + n_through),
            out_specs=list(out_specs) + [anywhere()] * n_through,
            scratch_shapes=scratch,
        ),
        out_shape=list(outs) + [jax.ShapeDtypeStruct(t.shape, t.dtype) for t in through],
        input_output_aliases={1 + n_in + n_after + i: n_out + i for i in range(n_through)},
        compiler_params=pltpu.CompilerParams(vmem_limit_bytes=limit * MIB),
        cost_estimate=pl.CostEstimate(flops=flops, transcendentals=0, bytes_accessed=moved),
        name=name,
    )(place, *operands, *after, *through)


def hold(value, *after):
    return pl.pallas_call(
        lambda *refs: None,
        in_specs=[anywhere()] * (1 + len(after)),
        out_specs=anywhere(),
        out_shape=jax.ShapeDtypeStruct(value.shape, value.dtype),
        input_output_aliases={0: 0},
        compiler_params=pltpu.CompilerParams(vmem_limit_bytes=MIB),
        name="hold",
    )(value, *after)


def row_copies(place, pieces, start_column, columns, whole, sems):
    part = pieces[0].shape[0] // SEQS
    copies = []
    for other in range(2):
        for across in range(2):
            core = (place[2] + other) % 2
            y = (place[1] + across) % 2
            for which in range(SEQS):
                start = pl.multiple_of(((which * 2 + core) * 2 + y) * part, part)
                copies.append(
                    pltpu.make_async_copy(
                        pieces[other * 2 + across].at[
                            pl.ds(which * part, part), pl.ds(start_column, columns)
                        ],
                        whole.at[pl.ds(start, part), :],
                        sems.at[len(copies)],
                    )
                )
    return copies


def start_all(copies):
    for copy in copies:
        copy.start()


def wait_all(copies):
    for copy in copies:
        copy.wait()


def down_kernel(steps, place, p0, p1, p2, p3, weight, gate, out, whole, row_sems):
    rows_in = row_copies(place, (p0, p1, p2, p3), 0, whole.shape[1], whole, row_sems)
    start_all(rows_in)
    wait_all(rows_in)
    depth = weight.shape[1] // steps
    total = None
    for i in range(steps):
        part = slice(i * depth, (i + 1) * depth)
        product = lax.dot_general(
            whole[:, part], weight[:, part], (((1,), (1,)), ((), ())), preferred_element_type=F32
        )
        total = product if total is None else total + product
    pre = gate[...]
    out[...] = (total * (pre / (1.0 + jnp.exp(-pre)))).astype(out.dtype)


def down_product(place, pieces, weight, gate, after, through, steps=4):
    rows, depth = pieces[0].shape
    width = weight.shape[0]
    return call(
        functools.partial(down_kernel, steps),
        place,
        (*pieces, weight, gate),
        [in_hbm()] * 4 + [pl.BlockSpec(memory_space=pltpu.VMEM)] * 2,
        [jax.ShapeDtypeStruct((4 * rows, width), BF16)],
        [same((4 * rows, width))],
        [pltpu.VMEM((4 * rows, depth), BF16), pltpu.SemaphoreType.DMA((4 * SEQS,))],
        8 * rows * depth * width,
        2 * rows * depth,
        "down",
        after=after,
        through=through,
        limit=16,
    )


def share_copies(place, basis, flip, block, buffer, sems):
    copies = []
    for chip in range(buffer.shape[0]):
        start = pl.multiple_of((2 * chip + (place[2] + flip) % 2) * block, block)
        copies.append(
            pltpu.make_async_copy(basis.at[:, pl.ds(start, block)], buffer.at[chip], sems.at[chip])
        )
    return copies


def share_products(left, copies, buffer, out):
    for chip, copy in enumerate(copies):
        copy.wait()
        out[chip] = jnp.dot(left[...], buffer[chip], preferred_element_type=F32).astype(out.dtype)


def front_kernel(steps, block, place, p0, p1, p2, p3, weight, basis, gate, send, keep, whole, left, buffer, buf0, buf1, sems, row_sems, left_sems, share_sems):
    pieces = (p0, p1, p2, p3)
    depth_a = left.shape[1]
    start = pl.multiple_of(place[3] * depth_a, depth_a)
    rows_in = row_copies(place, pieces, start, depth_a, left, left_sems)
    whole_in = row_copies(place, pieces, 0, whole.shape[1], whole, row_sems)
    sent = share_copies(place, basis, 1, block, buf0, share_sems.at[0])
    kept = share_copies(place, basis, 0, block, buf1, share_sems.at[1])
    depth = weight.shape[0] // steps
    copies = []
    for i in range(steps):
        rows = pl.ds(i * depth, depth)
        copies.append(pltpu.make_async_copy(weight.at[rows], buffer.at[rows], sems.at[i]))
    for some in (rows_in, sent, kept, whole_in, copies):
        start_all(some)
    wait_all(rows_in)
    share_products(left, sent, buf0, send)
    share_products(left, kept, buf1, keep)
    wait_all(whole_in)
    total = None
    for i in range(steps):
        copies[i].wait()
        part = slice(i * depth, (i + 1) * depth)
        product = jnp.dot(whole[:, part], buffer[part, :], preferred_element_type=F32)
        total = product if total is None else total + product
    gate[...] = total


def front(place, pieces, weight, basis, chips, after, steps=8):
    rows, depth = pieces[0].shape
    width = weight.shape[1]
    depth_a, columns = basis.shape
    block = columns // (2 * chips)
    shape = (chips, 4 * rows, block)
    return call(
        functools.partial(front_kernel, steps, block),
        place,
        (*pieces, weight, basis),
        [in_hbm()] * 6,
        [
            jax.ShapeDtypeStruct((4 * rows, width), F32),
            jax.ShapeDtypeStruct(shape, BF16),
            jax.ShapeDtypeStruct(shape, F32),
        ],
        [same((4 * rows, width)), same(shape), same(shape)],
        [
            pltpu.VMEM((4 * rows, depth), BF16),
            pltpu.VMEM((4 * rows, depth_a), BF16),
            pltpu.VMEM((depth, width), BF16),
            pltpu.VMEM((chips, depth_a, block), BF16),
            pltpu.VMEM((chips, depth_a, block), BF16),
            pltpu.SemaphoreType.DMA((steps,)),
            pltpu.SemaphoreType.DMA((4 * SEQS,)),
            pltpu.SemaphoreType.DMA((4 * SEQS,)),
            pltpu.SemaphoreType.DMA((2, chips)),
        ],
        8 * rows * (depth * width + depth_a * columns),
        2 * (depth * width + depth_a * columns),
        "front",
        after=after,
    )


def share_g_kernel(block, place, up, basis, send, keep, buf0, buf1, sems):
    sent = share_copies(place, basis, 1, block, buf0, sems.at[0])
    kept = share_copies(place, basis, 0, block, buf1, sems.at[1])
    start_all(sent)
    start_all(kept)
    share_products(up, sent, buf0, send)
    share_products(up, kept, buf1, keep)


def share_g(place, up, basis, chips, after, through):
    tokens, depth = up.shape
    block = basis.shape[1] // (2 * chips)
    shape = (chips, tokens, block)
    return call(
        functools.partial(share_g_kernel, block),
        place,
        (up, basis),
        [pl.BlockSpec(memory_space=pltpu.VMEM), in_hbm()],
        [jax.ShapeDtypeStruct(shape, BF16), jax.ShapeDtypeStruct(shape, F32)],
        [same(shape), same(shape)],
        [pltpu.VMEM((chips, depth, block), BF16)] * 2 + [pltpu.SemaphoreType.DMA((2, chips))],
        4 * tokens * depth * chips * block,
        4 * depth * chips * block,
        "share_g",
        after=after,
        through=through,
        limit=40,
    )


SLOTS = 8


def final_kernel(layers, place, a0, a1, a2, a3, g, out, pair, stage, sems):
    tokens, width = g.shape
    seq = tokens // SEQS
    block = stage.shape[1]
    pair[...] = jnp.zeros_like(pair)
    for s in range(SEQS):
        rows = slice(s * seq, (s + 1) * seq)
        pair[rows, s * width : (s + 1) * width] = g[rows, :]
    copies = []
    for step in range(4 * layers):
        which, z = divmod(step, layers)
        core = (place[2] + which // 2) % 2
        y = (place[1] + which) % 2
        slot = step % SLOTS
        if step >= SLOTS:
            copies[step - SLOTS].wait()
        product = lax.dot_general(
            (a0, a1, a2, a3)[which][z],
            pair[...],
            (((0,), (0,)), ((), ())),
            preferred_element_type=F32,
        )
        total = None
        for s in range(SEQS):
            one = product[:, s * width : (s + 1) * width]
            total = one * one if total is None else total + one * one
        stage[slot] = total * (1.0 / tokens)
        start = pl.multiple_of(((z * 2 + y) * 2 + core) * block, block)
        copies.append(
            pltpu.make_async_copy(stage.at[slot], out.at[pl.ds(start, block)], sems.at[slot])
        )
        copies[step].start()
    wait_all(copies[-SLOTS:])


def final_product(place, pieces, g):
    layers, tokens, block = pieces[0].shape
    width = g.shape[1]
    return call(
        functools.partial(final_kernel, layers),
        place,
        (*pieces, g),
        [pl.BlockSpec(memory_space=pltpu.VMEM)] * 5,
        [jax.ShapeDtypeStruct((4 * layers * block, width), F32)],
        [in_hbm()],
        [
            pltpu.VMEM((tokens, SEQS * width), BF16),
            pltpu.VMEM((SLOTS, block, width), F32),
            pltpu.SemaphoreType.DMA((SLOTS,)),
        ],
        8 * layers * block * width * tokens,
        16 * layers * block * width,
        "final",
        limit=24,
    )[0]


def turn(value, axis, size, by):
    return lax.ppermute(value, axis, [(i, (i + by) % size) for i in range(size)])


def from_z(value, layers):
    return [value] + [turn(value, "z", layers, by) for by in range(1, layers)]


def in_order(pieces, z):
    layers = len(pieces)
    return jnp.stack([lax.select_n((z - i) % layers, *pieces) for i in range(layers)])


def over_chip(mine):
    across = turn(mine, "y", 2, 1)
    return mine, across, turn(mine, "core", 2, 1), turn(across, "core", 2, 1)


def pick(value, which):
    return lax.dynamic_index_in_dim(value, which, 0, keepdims=False)


def for_y(keep, got, y, layers):
    shape = (layers, 2) + keep.shape[1:]
    keep, got = keep.reshape(shape), got.reshape(shape)

    def total(which):
        return lax.dynamic_index_in_dim(keep, which, 1, keepdims=False) + (
            lax.dynamic_index_in_dim(got, which, 1, keepdims=False).astype(F32)
        )

    return total(1 - y).astype(BF16), total(y)


def for_z(keep, got, z, layers):
    total = keep + got.astype(F32)
    return [pick(total, (z + by) % layers).astype(BF16) for by in range(1, layers)], pick(total, z)


def from_others(sends, layers):
    return [turn(send, "z", layers, by) for by, send in enumerate(sends, 1)]


def summed(keep, got):
    for one in got:
        keep = keep + one.astype(F32)
    return keep.astype(BF16)


def on_device(layers, activations, out_grad, loss_mask, w_gate, w_down, basis_a, basis_g):
    z, y, core = (lax.axis_index(name) for name in ("z", "y", "core"))
    chips = 2 * layers
    place = jnp.stack([z, y, core, lax.axis_index(("z", "y", "core"))]).astype(jnp.int32)
    masked = out_grad * loss_mask.astype(out_grad.dtype)[:, None]

    def flat(stacks):
        return [s.reshape(-1, s.shape[-1]) for s in stacks]

    w_down = pltpu.with_memory_space_constraint(w_down, pltpu.VMEM)
    act_z = in_order(from_z(activations, layers), z)
    grad_z = in_order(from_z(masked, layers), z)
    act = flat(over_chip(act_z))
    across = turn(grad_z, "y", 2, 1)
    gate, send_a, keep_a = front(place, act, w_gate, basis_a, chips, (grad_z,))
    across = hold(across, gate)
    send_a = hold(send_a, across)
    grad = flat((grad_z, across, turn(grad_z, "core", 2, 1), turn(across, "core", 2, 1)))
    send_a, keep_a = for_y(keep_a, turn(send_a, "core", 2, 1), y, layers)
    up, keep_a = down_product(place, grad, w_down, gate, (send_a,), (keep_a,))
    sends_a, own_a = for_z(keep_a, turn(send_a, "y", 2, 1), z, layers)
    send_g, keep_g, own_a = share_g(place, up, basis_g, chips, (sends_a[0],), (own_a,))
    own_a = summed(own_a, from_others(sends_a, layers))
    send_g = hold(send_g, own_a)
    send_g, keep_g = for_y(keep_g, turn(send_g, "core", 2, 1), y, layers)
    pieces_a = from_z(own_a, layers)
    sends_g, own_g = for_z(keep_g, turn(send_g, "y", 2, 1), z, layers)
    own_g = summed(own_g, from_others(sends_g, layers))
    pieces_a[0] = hold(own_a, sends_g[0])
    mine = in_order(pieces_a, z)
    across = hold(turn(mine, "y", 2, 1), own_g)
    proj_a = mine, across, turn(mine, "core", 2, 1), turn(across, "core", 2, 1)
    return final_product(place, proj_a, own_g)


def solution(mesh):
    tensor = mesh.shape["tensor"]
    chips = tensor // 2
    across = max(d for d in range(1, chips + 1) if chips % d == 0 and d * d <= chips)
    layers = chips // across
    fine = Mesh(
        mesh.devices.reshape(mesh.shape["parts"], layers, across, 2), ("parts", "z", "y", "core")
    )
    t = ("z", "y", "core")
    placed = (
        P(("parts",) + t, None),
        P(("parts",) + t, None),
        P(("parts",) + t),
        P(None, t),
        P(t, None),
        P(t, None),
        P(t, None),
    )

    def step(*args):
        rows = args[0].shape[0] // (mesh.shape["parts"] * tensor)
        small = across == 2 and layers * rows // SEQS == 16
        body = functools.partial(on_device, layers) if small else plain
        return jax.shard_map(
            body, mesh=fine, in_specs=placed, out_specs=P("parts", t), check_vma=False
        )(*args)

    return step
```
